32 devices in a mesh: replica: 2 (over x), outer: 4 (over y, core), link: 4 (over z).
Axes of the slice: x: 2, y: 2, z: 4, core: 2. Of those that a mesh axis runs over, the one named last changes fastest.
Arguments:
- link_in: bfloat16 [2, 8192, 256], P('replica', ('outer', 'link')), may hold values from -6 to 6
- path_in: bfloat16 [2, 2048, 256], P('replica', ('outer', 'link')), may hold values from -6 to 6
- hop_slots: int32 [2, 2048, 24], P('replica', ('outer', 'link')), may hold values from 0 to 1023
- hop_lens: int32 [2, 2048], P('replica', ('outer', 'link')), may hold values from 2 to 24
- failed: int32 [2, 8192], P('replica', ('outer', 'link')), may hold values 0 or 1
- serve_index: int32 [2, 16, 16, 64], P('replica', None, ('outer', 'link')), may hold values from 0 to 511
- link_grad: bfloat16 [2, 8192, 256], P('replica', ('outer', 'link')), may hold values from -6 to 6
- path_grad: bfloat16 [2, 2048, 256], P('replica', ('outer', 'link')), may hold values from -6 to 6
- gru_wx: bfloat16 [256, 768], replicated, may hold values from -0.375 to 0.375
- gru_wh: bfloat16 [256, 768], replicated, may hold values from -0.375 to 0.375
- gru_bias: float32 [768], replicated, may hold values from -3 to 3
- mlp_w1: bfloat16 [512, 256], replicated, may hold values from -0.25 to 0.25
- mlp_b1: float32 [256], replicated, may hold values from -3 to 3
- mlp_w2: bfloat16 [256, 256], replicated, may hold values from -0.375 to 0.375
- mlp_b2: float32 [256], replicated, may hold values from -3 to 3
Outputs:
- link_out: bfloat16 [2, 8192, 256], P('replica', ('outer', 'link'))
- path_out: bfloat16 [2, 2048, 256], P('replica', ('outer', 'link'))
- link_in_grad: float32 [2, 8192, 256], P('replica', ('outer', 'link'))
- path_in_grad: float32 [2, 2048, 256], P('replica', ('outer', 'link'))
- grad_wx: float32 [256, 768], replicated
- grad_wh: float32 [256, 768], replicated
- grad_bias: float32 [768], replicated
- grad_w1: float32 [512, 256], replicated
- grad_b1: float32 [256], replicated
- grad_w2: float32 [256, 256], replicated
- grad_b2: float32 [256], replicated
The draws below stay inside these ranges and needn't reach their ends.
Inputs may be any that keep to these rules, and one draw needn't show every extreme that they name: `serve_index`: entry [s, d, o, c] names, among the 512 links of owner device o, the link in request slot c of device d; a link may fill several slots. `hop_slots`: slot o * 64 + c is request slot c of the flow's own device towards owner o; entries at hops past the flow's length are ignored. 1 marks a failed link.
All inputs are finite; a program needn't handle non-finite values. No bound on the sum of `failed` on one device may be relied on, other than what follows from the above.
Results may differ from the reference program's by a relative error of at most 0.0067.
Values may be sent and summed in bfloat16 or wider, within the bound.
A program may use at most 128 MiB of HBM per device.

```python
import math
import jax
import jax.numpy as jnp
import numpy as np
from jax import lax

D = 256
H = 24
F_DEV = 128
L_DEV = 512
GROUP = 16
CAP = 64
SCEN = 2
LINKS = 8192
FLOWS = 2048


def place_ends(drawn, rng, low, largest):
    place = [jax.random.randint(jax.random.fold_in(rng, axis), (), 0, length) for axis, length in enumerate(drawn.shape)]
    longest = drawn.shape.index(max(drawn.shape))
    next_to = place[:longest] + [(place[longest] + 1) % drawn.shape[longest]] + place[longest + 1:]
    return drawn.at[tuple(place)].set(low).at[tuple(next_to)].set(largest)


def levels(stream_key, extent, cuts, smallest, largest):
    gain = 1.0
    for dim, shards_of in cuts:
        draws = jax.random.uniform(jax.random.fold_in(jax.random.fold_in(stream_key, 6), dim), (shards_of,), jnp.float32, smallest / len(cuts), largest / len(cuts))
        gain = gain * jnp.repeat(jnp.exp(draws), extent[dim] // shards_of).reshape((-1,) + (1,) * (len(extent) - 1 - dim))
    return gain


def rank_table(count, slope):
    weights = [(1 << 20) // math.isqrt(standing ** slope) + 1 for standing in range(1, count + 1)]
    spread = 1 + sum(weights) // (1 << 30)
    return np.cumsum(np.array([max(1, weight // spread) for weight in weights]))


def skewed_ids(rng, dims, amount, skew):
    listing = rank_table(amount, skew)
    lot = jax.random.randint(jax.random.fold_in(rng, 1), dims, 0, int(listing[amount - 1]))
    rank = jnp.searchsorted(jnp.asarray(listing, jnp.int32), lot, side="right")
    return jax.random.permutation(jax.random.fold_in(rng, 2), amount)[rank].astype(jnp.int32)


def noise(stream_key, dims, spread, bound, pieces=(), held_as=jnp.bfloat16):
    loudness = levels(stream_key, dims, pieces, -0.22, 0.18) if pieces else 1.0
    values = jax.random.normal(stream_key, dims, jnp.float32) * spread * loudness
    return jnp.minimum(jnp.maximum(values, -bound), bound).astype(held_as)


def setup_inputs(seed: int = 0) -> dict:
    key_of = jax.random.split(jax.random.key(seed), 16)
    link_in = noise(key_of[0], (SCEN, LINKS, D), 1.0, 6.0, ((0, 2), (1, 16)))
    path_in = noise(key_of[1], (SCEN, FLOWS, D), 1.0, 6.0, ((0, 2), (1, 16)))
    hop_slots = place_ends(skewed_ids(key_of[2], (SCEN, FLOWS, H), GROUP * CAP, 1), jax.random.fold_in(key_of[2], 3), 0, (GROUP * CAP) - 1).astype(jnp.int32)
    hop_lens = place_ends(jax.random.randint(key_of[3], (SCEN, FLOWS), 2, H + 1), jax.random.fold_in(key_of[3], 1), 2, H).astype(jnp.int32)
    failed = place_ends((jax.random.randint(key_of[4], (SCEN, LINKS), 0, 16) < 1).astype(jnp.int32), jax.random.fold_in(key_of[4], 1), 0, 1)
    serve_index = place_ends(jax.random.randint(key_of[5], (SCEN, GROUP, GROUP, CAP), 0, L_DEV), jax.random.fold_in(key_of[5], 1), 0, L_DEV - 1).astype(jnp.int32)
    link_grad = noise(key_of[6], (SCEN, LINKS, D), 1.0, 6.0, ((0, 2), (1, 16)))
    path_grad = noise(key_of[7], (SCEN, FLOWS, D), 1.0, 6.0, ((0, 2), (1, 16)))
    gru_wx = noise(key_of[8], (D, 3 * D), D ** -0.5, 0.375)
    gru_wh = noise(key_of[9], (D, 3 * D), D ** -0.5, 0.375)
    gru_bias = noise(key_of[10], (3 * D,), 0.5, 3.0, (), jnp.float32)
    mlp_w1 = noise(key_of[11], (2 * D, D), (2 * D) ** -0.5, 0.25)
    mlp_b1 = noise(key_of[12], (D,), 0.5, 3.0, (), jnp.float32)
    mlp_w2 = noise(key_of[13], (D, D), D ** -0.5, 0.375)
    mlp_b2 = noise(key_of[14], (D,), 0.5, 3.0, (), jnp.float32)
    return {"link_in": link_in, "path_in": path_in, "hop_slots": hop_slots, "hop_lens": hop_lens, "failed": failed, "serve_index": serve_index, "link_grad": link_grad, "path_grad": path_grad, "gru_wx": gru_wx, "gru_wh": gru_wh, "gru_bias": gru_bias, "mlp_w1": mlp_w1, "mlp_b1": mlp_b1, "mlp_w2": mlp_w2, "mlp_b2": mlp_b2}


def gate_terms(state_now, hop_input, input_weight, hidden_weight, gate_bias):
    from_input = jnp.dot(hop_input, input_weight, preferred_element_type=jnp.float32) + gate_bias
    from_state = jnp.dot(state_now.astype(jnp.bfloat16), hidden_weight, preferred_element_type=jnp.float32)
    return from_input, from_state


def gru_cell(state_now, from_input, from_state):
    feat_width = state_now.shape[1]
    update = jax.nn.sigmoid(from_input[:, :feat_width] + from_state[:, :feat_width])
    reset = jax.nn.sigmoid(from_input[:, feat_width:2 * feat_width] + from_state[:, feat_width:2 * feat_width])
    candidate = jnp.tanh(from_input[:, 2 * feat_width:] + reset * from_state[:, 2 * feat_width:])
    return candidate + update * (state_now - candidate), update, reset, candidate


def gru_forward(path_start, hop_inputs, live_mask, input_weight, hidden_weight, gate_bias, keep_gates):
    def advance(state_now, scan_item):
        hop_input, live_now = scan_item
        from_input, from_state = gate_terms(state_now, hop_input, input_weight, hidden_weight, gate_bias)
        stepped = gru_cell(state_now, from_input, from_state)[0]
        state_next = jnp.where(live_now[:, None] > 0, stepped, state_now)
        if keep_gates:
            return state_next, (state_next, from_input, from_state)
        return state_next, (state_next,)
    return lax.scan(advance, path_start.astype(jnp.float32), (hop_inputs, live_mask))[1]


def back_step(carried, hop_input, state_now, live_now, hop_grad, from_input, from_state, input_tr, hidden_tr):
    grad_state, grad_wx, grad_wh, grad_bias = carried
    feat_width = state_now.shape[1]
    live_col = live_now[:, None]
    grad_state = grad_state + live_col * hop_grad
    update, reset, candidate = gru_cell(state_now, from_input, from_state)[1:]
    pre_update = grad_state * (state_now - candidate) * update * (1.0 - update)
    pre_cand = grad_state * (1.0 - update) * (1.0 - candidate * candidate)
    pre_reset = pre_cand * from_state[:, 2 * feat_width:] * reset * (1.0 - reset)
    grad_in = jnp.concatenate([pre_update, pre_reset, pre_cand], axis=1) * live_col
    grad_hid = jnp.concatenate([pre_update, pre_reset, pre_cand * reset], axis=1) * live_col
    in_bf = grad_in.astype(jnp.bfloat16)
    hid_bf = grad_hid.astype(jnp.bfloat16)
    grad_prev = jnp.where(live_col > 0, grad_state * update + jnp.dot(hid_bf, hidden_tr, preferred_element_type=jnp.float32), grad_state)
    grad_input = jnp.dot(in_bf, input_tr, preferred_element_type=jnp.float32)
    grad_wx = grad_wx + jnp.dot(hop_input.T, in_bf, preferred_element_type=jnp.float32)
    grad_wh = grad_wh + jnp.dot(state_now.astype(jnp.bfloat16).T, hid_bf, preferred_element_type=jnp.float32)
    grad_bias = grad_bias + jnp.sum(grad_in, axis=0)
    return (grad_prev, grad_wx, grad_wh, grad_bias), grad_input


def gru_backward(path_start, states, hop_inputs, live_mask, hop_grads, path_grad, input_weight, hidden_weight, gate_bias, kept):
    feat_width = path_start.shape[1]
    prior_states = jnp.concatenate([path_start.astype(jnp.float32)[None], states[:-1]], axis=0)
    input_tr = input_weight.T
    hidden_tr = hidden_weight.T
    initial = (path_grad.astype(jnp.float32), jnp.zeros((feat_width, 3 * feat_width), jnp.float32),
               jnp.zeros((feat_width, 3 * feat_width), jnp.float32), jnp.zeros((3 * feat_width,), jnp.float32))
    if kept is None:
        def retreat(carried, scan_item):
            hop_input, state_now, live_now, hop_grad = scan_item
            from_input, from_state = gate_terms(state_now, hop_input, input_weight, hidden_weight, gate_bias)
            return back_step(carried, hop_input, state_now, live_now, hop_grad, from_input, from_state, input_tr, hidden_tr)
        scan_items = (hop_inputs, prior_states, live_mask, hop_grads)
    else:
        def retreat(carried, scan_item):
            hop_input, state_now, live_now, hop_grad, from_input, from_state = scan_item
            return back_step(carried, hop_input, state_now, live_now, hop_grad, from_input, from_state, input_tr, hidden_tr)
        scan_items = (hop_inputs, prior_states, live_mask, hop_grads, kept[0], kept[1])
    return lax.scan(retreat, initial, scan_items, reverse=True)


def link_forward(link_rows, agg_bf, keep_col, mlp_w1, mlp_b1, mlp_w2, mlp_b2):
    feat_width = link_rows.shape[1]
    pre_act = (jnp.dot(link_rows, mlp_w1[:feat_width], preferred_element_type=jnp.float32)
               + jnp.dot(agg_bf, mlp_w1[feat_width:], preferred_element_type=jnp.float32) + mlp_b1)
    activ = jax.nn.silu(pre_act).astype(jnp.bfloat16)
    value = link_rows.astype(jnp.float32) + jnp.dot(activ, mlp_w2, preferred_element_type=jnp.float32) + mlp_b2
    return (keep_col * value).astype(jnp.bfloat16), pre_act, activ


def link_backward(link_grad_rows, link_rows, agg_bf, keep_col, pre_act, activ, mlp_w1, mlp_w2):
    feat_width = link_rows.shape[1]
    grad_val = keep_col * link_grad_rows.astype(jnp.float32)
    val_bf = grad_val.astype(jnp.bfloat16)
    grad_w2 = jnp.dot(activ.T, val_bf, preferred_element_type=jnp.float32)
    grad_b2 = jnp.sum(grad_val, axis=0)
    grad_act = jnp.dot(val_bf, mlp_w2.T, preferred_element_type=jnp.float32)
    sigma = jax.nn.sigmoid(pre_act)
    grad_pre = grad_act * sigma * (1.0 + pre_act * (1.0 - sigma))
    pre_bf = grad_pre.astype(jnp.bfloat16)
    grad_w1 = jnp.concatenate([jnp.dot(link_rows.T, pre_bf, preferred_element_type=jnp.float32),
                               jnp.dot(agg_bf.T, pre_bf, preferred_element_type=jnp.float32)], axis=0)
    grad_b1 = jnp.sum(grad_pre, axis=0)
    link_direct = grad_val + jnp.dot(pre_bf, mlp_w1[:feat_width].T, preferred_element_type=jnp.float32)
    agg_grad = jnp.dot(pre_bf, mlp_w1[feat_width:].T, preferred_element_type=jnp.float32).astype(jnp.bfloat16)
    return link_direct, agg_grad, (grad_w1, grad_b1, grad_w2, grad_b2)


def reference(link_in, path_in, hop_slots, hop_lens, failed, serve_index, link_grad, path_grad, gru_wx, gru_wh, gru_bias, mlp_w1, mlp_b1, mlp_w2, mlp_b2):
    slot_count = GROUP * CAP
    owner_base = (jnp.arange(GROUP, dtype=jnp.int32) * L_DEV)[None, :, None]
    hop_range = jnp.arange(H, dtype=jnp.int32)
    flow_device = jnp.arange(FLOWS, dtype=jnp.int32) // F_DEV

    def scenario(carried, scan_item):
        links_s, paths_s, slots_s, lens_s, failed_s, serve_s, lgrad_s, pgrad_s = scan_item
        glink = (serve_s + owner_base).reshape(GROUP * slot_count).astype(jnp.int32)
        key_rows = (flow_device[:, None] * slot_count + slots_s).T.astype(jnp.int32)
        link_ids = glink[key_rows]
        live_mask = (hop_range[:, None] < lens_s[None, :]).astype(jnp.float32)
        hop_inputs = links_s[link_ids]
        states, from_inputs, from_states = gru_forward(paths_s, hop_inputs, live_mask, gru_wx, gru_wh, gru_bias, True)
        partial_value = jax.ops.segment_sum((states * live_mask[:, :, None]).reshape(H * FLOWS, D), key_rows.reshape(-1),
                                      num_segments=GROUP * slot_count).astype(jnp.bfloat16)
        aggregate = jax.ops.segment_sum(partial_value.astype(jnp.float32), glink, num_segments=LINKS)
        agg_bf = aggregate.astype(jnp.bfloat16)
        keep_col = (1 - failed_s).astype(jnp.float32)[:, None]
        link_out, pre_act, activ = link_forward(links_s, agg_bf, keep_col, mlp_w1, mlp_b1, mlp_w2, mlp_b2)
        path_out = states[-1].astype(jnp.bfloat16)
        link_direct, agg_grad, mlp_terms = link_backward(lgrad_s, links_s, agg_bf, keep_col, pre_act, activ, mlp_w1, mlp_w2)
        hop_grads = agg_grad[link_ids].astype(jnp.float32) * live_mask[:, :, None]
        finished, grad_inputs = gru_backward(paths_s, states, hop_inputs, live_mask, hop_grads, pgrad_s,
                                             gru_wx, gru_wh, gru_bias, (from_inputs, from_states))
        dpart = jax.ops.segment_sum(grad_inputs.reshape(H * FLOWS, D), key_rows.reshape(-1),
                                    num_segments=GROUP * slot_count).astype(jnp.bfloat16)
        link_back = link_direct + jax.ops.segment_sum(dpart.astype(jnp.float32), glink, num_segments=LINKS)
        terms = (finished[1], finished[2], finished[3]) + mlp_terms
        summed = tuple(total + term for total, term in zip(carried, terms))
        return summed, (link_out, path_out, link_back, finished[0])

    zero_grads = (jnp.zeros((D, 3 * D), jnp.float32), jnp.zeros((D, 3 * D), jnp.float32), jnp.zeros((3 * D,), jnp.float32),
                  jnp.zeros((2 * D, D), jnp.float32), jnp.zeros((D,), jnp.float32), jnp.zeros((D, D), jnp.float32),
                  jnp.zeros((D,), jnp.float32))
    grads, (link_out, path_out, link_back, path_back) = lax.scan(
        scenario, zero_grads, (link_in, path_in, hop_slots, hop_lens, failed, serve_index, link_grad, path_grad))
    grad_scale = float(SCEN * LINKS) ** -0.5
    return (link_out, path_out, link_back, path_back, grads[0] * grad_scale, grads[1] * grad_scale, grads[2] * grad_scale,
            grads[3] * grad_scale, grads[4] * grad_scale, grads[5] * grad_scale, grads[6] * grad_scale)
```

```python
import functools

import jax
import jax.numpy as jnp
from jax import lax
from jax.experimental import pallas as pl
from jax.experimental.pallas import tpu as pltpu
from jax.sharding import PartitionSpec as P

VMEM_BYTES = 56 * 1024 * 1024


def mm(a, b):
    return jnp.dot(a, b, preferred_element_type=jnp.float32)


def mm_nt(a, b):
    return lax.dot_general(a, b, (((1,), (1,)), ((), ())), preferred_element_type=jnp.float32)


def mm_tn(a, b):
    return lax.dot_general(a, b, (((0,), (0,)), ((), ())), preferred_element_type=jnp.float32)


def sigmoid(v):
    return 0.5 * jnp.tanh(0.5 * v) + 0.5


def one_hot_rows(col, width):
    ids = lax.broadcasted_iota(jnp.int32, (col.shape[0], width), 1)
    return jnp.where(ids == col, 1.0, 0.0).astype(jnp.bfloat16)


def one_hot_cols(row, height):
    ids = lax.broadcasted_iota(jnp.int32, (height, row.shape[1]), 0)
    return jnp.where(ids == row, 1.0, 0.0).astype(jnp.bfloat16)


def whole(memory_space=pltpu.VMEM):
    return pl.BlockSpec(memory_space=memory_space)


def serve_kernel(col_ref, link_ref, out_ref):
    hot = one_hot_rows(col_ref[...], link_ref.shape[0])
    out_ref[...] = mm(hot, link_ref[...]).astype(jnp.bfloat16)


def forward_kernel(
    steps,
    fetched_ref,
    path_ref,
    col_ref,
    row_ref,
    lens_ref,
    wx_ref,
    wh_ref,
    bias_ref,
    xs_ref,
    hs_ref,
    coef_ref,
    partial_ref,
    path_out_ref,
    state,
    total,
    from_input,
    reached,
):
    block = pl.program_id(0)
    flows, width = path_ref.shape
    slots = fetched_ref.shape[0]

    @pl.when(block == 0)
    def _():
        state[...] = path_ref[...].astype(jnp.float32)
        total[...] = jnp.zeros_like(total)

    x = mm(one_hot_rows(col_ref[...], slots), fetched_ref[...]).astype(jnp.bfloat16)
    xs_ref[...] = x
    from_input[...] = mm(x, wx_ref[...]) + bias_ref[...]
    h = state[...]
    for u in range(steps):
        rows = pl.ds(u * flows, flows)
        live = lens_ref[...] > block * steps + u
        h_bf = h.astype(jnp.bfloat16)
        hs_ref[rows, :] = h_bf
        gs = mm(h_bf, wh_ref[...])
        gi = from_input[rows, :]
        z = sigmoid(gi[:, :width] + gs[:, :width])
        r = sigmoid(gi[:, width : 2 * width] + gs[:, width : 2 * width])
        gs3 = gs[:, 2 * width :]
        n = jnp.tanh(gi[:, 2 * width :] + r * gs3)
        diff = h - n
        h = jnp.where(live, n + z * diff, h)
        reached[rows, :] = jnp.where(live, h, 0.0).astype(jnp.bfloat16)
        rest = 1.0 - z
        c_n = jnp.where(live, rest * (1.0 - n * n), 0.0)
        coef_ref[rows, :width] = jnp.where(live, diff * z * rest, 0.0)
        coef_ref[rows, width : 2 * width] = c_n * gs3 * r * (1.0 - r)
        coef_ref[rows, 2 * width : 3 * width] = c_n
        coef_ref[rows, 3 * width : 4 * width] = c_n * r
        coef_ref[rows, 4 * width :] = jnp.where(live, z, 1.0)
    state[...] = h
    total[...] += mm(one_hot_cols(row_ref[0], slots), reached[...])

    @pl.when(block == pl.num_programs(0) - 1)
    def _():
        partial_ref[...] = total[...].astype(jnp.bfloat16)
        path_out_ref[...] = state[...].astype(jnp.bfloat16)


def link_kernel(
    arrived_ref,
    row_ref,
    col_ref,
    link_ref,
    grad_ref,
    keep_ref,
    w1_ref,
    b1_ref,
    w2_ref,
    b2_ref,
    link_out_ref,
    direct_ref,
    back_ref,
    grad_w_ref,
    grad_b_ref,
):
    links, width = link_ref.shape
    rows = link_ref[...]
    keep = keep_ref[...]
    agg = mm(one_hot_cols(row_ref[...], links), arrived_ref[...]).astype(jnp.bfloat16)
    u = mm(rows, w1_ref[:width, :]) + mm(agg, w1_ref[width:, :]) + b1_ref[...]
    s = sigmoid(u)
    act = (u * s).astype(jnp.bfloat16)
    value = rows.astype(jnp.float32) + mm(act, w2_ref[...]) + b2_ref[...]
    link_out_ref[...] = (keep * value).astype(jnp.bfloat16)
    gv = keep * grad_ref[...].astype(jnp.float32)
    gv_bf = gv.astype(jnp.bfloat16)
    du = mm_nt(gv_bf, w2_ref[...]) * s * (1.0 + u * (1.0 - s))
    du_bf = du.astype(jnp.bfloat16)
    d_agg = mm_nt(du_bf, w1_ref[width:, :]).astype(jnp.bfloat16)
    back_ref[...] = mm(one_hot_rows(col_ref[...], links), d_agg).astype(jnp.bfloat16)
    direct_ref[...] = gv + mm_nt(du_bf, w1_ref[:width, :])
    grad_w_ref[:width, :] = mm_tn(rows, du_bf)
    grad_w_ref[width : 2 * width, :] = mm_tn(agg, du_bf)
    grad_w_ref[2 * width :, :] = mm_tn(act, gv_bf)
    grad_b_ref[0:1, :] = jnp.sum(du, axis=0, keepdims=True)
    grad_b_ref[1:2, :] = jnp.sum(gv, axis=0, keepdims=True)


def backward_kernel(
    steps,
    returned_ref,
    path_grad_ref,
    col_ref,
    row_ref,
    lens_ref,
    wx_ref,
    wh_ref,
    xs_ref,
    hs_ref,
    coef_ref,
    dpart_ref,
    path_back_ref,
    grad_wx_ref,
    grad_wh_ref,
    grad_b_ref,
    carry,
    total,
    hop_grad,
    dgi,
    dgs,
    acc_wx,
    acc_wh,
    acc_b,
):
    block = pl.num_programs(0) - 1 - pl.program_id(0)
    flows, width = path_grad_ref.shape
    slots = returned_ref.shape[0]

    @pl.when(pl.program_id(0) == 0)
    def _():
        carry[...] = path_grad_ref[...].astype(jnp.float32)
        total[...] = jnp.zeros_like(total)
        acc_wx[...] = jnp.zeros_like(acc_wx)
        acc_wh[...] = jnp.zeros_like(acc_wh)
        acc_b[...] = jnp.zeros_like(acc_b)

    hop_grad[...] = mm(one_hot_rows(col_ref[...], slots), returned_ref[...])
    g = carry[...]
    for u in reversed(range(steps)):
        rows = pl.ds(u * flows, flows)
        live = lens_ref[...] > block * steps + u
        g = g + jnp.where(live, hop_grad[rows, :], 0.0)
        a_z = g * coef_ref[rows, :width]
        a_r = g * coef_ref[rows, width : 2 * width]
        a_n = g * coef_ref[rows, 2 * width : 3 * width]
        a_h = g * coef_ref[rows, 3 * width : 4 * width]
        z_bf = a_z.astype(jnp.bfloat16)
        r_bf = a_r.astype(jnp.bfloat16)
        dgs[rows, :width] = z_bf
        dgs[rows, width : 2 * width] = r_bf
        dgs[rows, 2 * width :] = a_h.astype(jnp.bfloat16)
        g = g * coef_ref[rows, 4 * width :] + mm_nt(dgs[rows, :], wh_ref[...])
        dgi[rows, :width] = z_bf
        dgi[rows, width : 2 * width] = r_bf
        dgi[rows, 2 * width :] = a_n.astype(jnp.bfloat16)
        for k, a in enumerate((a_z, a_r, a_n)):
            folded = jnp.sum(a.reshape(flows // 8, 8, width), axis=0)
            acc_b[:, k * width : (k + 1) * width] += folded
    carry[...] = g
    dx = mm_nt(dgi[...], wx_ref[...]).astype(jnp.bfloat16)
    total[...] += mm(one_hot_cols(row_ref[0], slots), dx)
    acc_wx[...] += mm_tn(xs_ref[...], dgi[...])
    acc_wh[...] += mm_tn(hs_ref[...], dgs[...])

    @pl.when(pl.program_id(0) == pl.num_programs(0) - 1)
    def _():
        dpart_ref[...] = total[...].astype(jnp.bfloat16)
        path_back_ref[...] = carry[...]
        emit_grads(acc_wx, acc_wh, acc_b, grad_wx_ref, grad_wh_ref, grad_b_ref)


def collect_kernel(owned_ref, row_ref, direct_ref, out_ref):
    hot = one_hot_cols(row_ref[...], direct_ref.shape[0])
    out_ref[...] = direct_ref[...] + mm(hot, owned_ref[...])


def call(kernel, out_shapes, **options):
    return pl.pallas_call(
        kernel,
        out_shape=[jax.ShapeDtypeStruct(shape, dtype) for shape, dtype in out_shapes],
        compiler_params=pltpu.CompilerParams(vmem_limit_bytes=VMEM_BYTES),
        **options,
    )


def emit_grads(acc_wx, acc_wh, acc_b, grad_wx_ref, grad_wh_ref, grad_b_ref):
    grad_wx_ref[...] = acc_wx[...]
    grad_wh_ref[...] = acc_wh[...]
    grad_b_ref[...] = jnp.sum(acc_b[...], axis=0, keepdims=True)


def swap_slots(rows, group, cap):
    blocks = rows.reshape(group, cap, rows.shape[1])
    moved = lax.all_to_all(blocks, ("outer", "link"), split_axis=0, concat_axis=0, tiled=True)
    return moved.reshape(group * cap, rows.shape[1])


def body(
    link_in,
    path_in,
    hop_slots,
    hop_lens,
    failed,
    serve_index,
    link_grad,
    path_grad,
    gru_wx,
    gru_wh,
    gru_bias,
    mlp_w1,
    mlp_b1,
    mlp_w2,
    mlp_b2,
):
    bf, f32 = jnp.bfloat16, jnp.float32
    link_rows = link_in[0]
    links, width = link_rows.shape
    serve_rows = serve_index[0, :, 0, :]
    group, cap = serve_rows.shape
    slots = group * cap
    serve_row = serve_rows.reshape(1, slots)
    serve_col = serve_rows.reshape(slots, 1)
    flows, hops = hop_slots.shape[1:]
    steps = 4 if hops % 4 == 0 else 1
    blocks = hops // steps
    slot_ids = hop_slots[0].T
    slot_col = slot_ids.reshape(hops * flows, 1)
    slot_row = slot_ids.reshape(blocks, 1, steps * flows)
    lens_col = hop_lens[0].reshape(flows, 1)
    keep_col = (1 - failed[0]).astype(f32)[:, None]
    span = steps * flows

    served = call(
        serve_kernel, [((slots, width), bf)], in_specs=[whole()] * 2, out_specs=[whole()]
    )(serve_col, link_rows)[0]
    fetched = swap_slots(served, group, cap)

    def fixed(*shape):
        return pl.BlockSpec(shape, lambda i: (0,) * len(shape))

    def ahead(*shape):
        return pl.BlockSpec(shape, lambda i: (i,) + (0,) * (len(shape) - 1))

    def behind(*shape):
        return pl.BlockSpec(shape, lambda i: (blocks - 1 - i,) + (0,) * (len(shape) - 1))

    xs, hs, coef, partial_value, path_out = call(
        functools.partial(forward_kernel, steps),
        [
            ((hops * flows, width), bf),
            ((hops * flows, width), bf),
            ((hops * flows, 5 * width), f32),
            ((slots, width), bf),
            ((flows, width), bf),
        ],
        grid=(blocks,),
        in_specs=[
            fixed(slots, width),
            fixed(flows, width),
            ahead(span, 1),
            ahead(1, 1, span),
            fixed(flows, 1),
            fixed(width, 3 * width),
            fixed(width, 3 * width),
            fixed(1, 3 * width),
        ],
        out_specs=[
            ahead(span, width),
            ahead(span, width),
            ahead(span, 5 * width),
            fixed(slots, width),
            fixed(flows, width),
        ],
        scratch_shapes=[
            pltpu.VMEM((flows, width), f32),
            pltpu.VMEM((slots, width), f32),
            pltpu.VMEM((span, 3 * width), f32),
            pltpu.VMEM((span, width), bf),
        ],
    )(fetched, path_in[0], slot_col, slot_row, lens_col, gru_wx, gru_wh, gru_bias[None])
    arrived = swap_slots(partial_value, group, cap)

    link_out, direct, back, grad_w, grad_b = call(
        link_kernel,
        [
            ((links, width), bf),
            ((links, width), f32),
            ((slots, width), bf),
            ((3 * width, width), f32),
            ((2, width), f32),
        ],
        in_specs=[whole()] * 10,
        out_specs=[whole()] * 5,
    )(
        arrived,
        serve_row,
        serve_col,
        link_rows,
        link_grad[0],
        keep_col,
        mlp_w1,
        mlp_b1[None],
        mlp_w2,
        mlp_b2[None],
    )
    returned = swap_slots(back, group, cap)

    dpart, path_back, grad_wx, grad_wh, grad_bias = call(
        functools.partial(backward_kernel, steps),
        grad_shapes(slots, flows, width),
        grid=(blocks,),
        in_specs=[
            fixed(slots, width),
            fixed(flows, width),
            behind(span, 1),
            behind(1, 1, span),
            fixed(flows, 1),
            fixed(width, 3 * width),
            fixed(width, 3 * width),
            behind(span, width),
            behind(span, width),
            behind(span, 5 * width),
        ],
        out_specs=[fixed(*shape) for shape, _ in grad_shapes(slots, flows, width)],
        scratch_shapes=[
            pltpu.VMEM((flows, width), f32),
            pltpu.VMEM((slots, width), f32),
            pltpu.VMEM((span, width), f32),
            pltpu.VMEM((span, 3 * width), bf),
            pltpu.VMEM((span, 3 * width), bf),
            pltpu.VMEM((width, 3 * width), f32),
            pltpu.VMEM((width, 3 * width), f32),
            pltpu.VMEM((8, 3 * width), f32),
        ],
    )(
        returned,
        path_grad[0],
        slot_col,
        slot_row,
        lens_col,
        gru_wx,
        gru_wh,
        xs,
        hs,
        coef,
    )
    everywhere = ("replica", "outer", "link")
    devices = lax.axis_size("replica") * lax.axis_size("outer") * lax.axis_size("link")
    scale = float(devices * links) ** (-0.5)
    owned, total_wx, total_wh, total_b, total_w, total_wb = finish(
        dpart, grad_wx, grad_wh, grad_bias, grad_w, grad_b, group, cap, scale, everywhere
    )
    link_back = call(
        collect_kernel, [((links, width), f32)], in_specs=[whole()] * 3, out_specs=[whole()]
    )(owned, serve_row, direct)[0]
    return (
        link_out[None],
        path_out[None],
        link_back[None],
        path_back[None],
        total_wx,
        total_wh,
        total_b,
        total_w[: 2 * width],
        total_wb[0],
        total_w[2 * width :],
        total_wb[1],
    )


def grad_shapes(slots, flows, width):
    return [
        ((slots, width), jnp.bfloat16),
        ((flows, width), jnp.float32),
        ((width, 3 * width), jnp.float32),
        ((width, 3 * width), jnp.float32),
        ((1, 3 * width), jnp.float32),
    ]


def finish(
    dpart, grad_wx, grad_wh, grad_bias, grad_w, grad_b, group, cap, scale, everywhere
):
    total_w, total_wb = lax.psum((grad_w, grad_b), everywhere)
    owned = swap_slots(dpart, group, cap)
    total_wx, total_wh, total_b = lax.psum((grad_wx, grad_wh, grad_bias[0]), everywhere)
    return (
        owned,
        total_wx * scale,
        total_wh * scale,
        total_b * scale,
        total_w * scale,
        total_wb * scale,
    )


def solution(mesh):
    return jax.shard_map(
        body,
        mesh=mesh,
        in_specs=(
            P("replica", ("outer", "link"), None),
            P("replica", ("outer", "link"), None),
            P("replica", ("outer", "link"), None),
            P("replica", ("outer", "link")),
            P("replica", ("outer", "link")),
            P("replica", None, ("outer", "link"), None),
            P("replica", ("outer", "link"), None),
            P("replica", ("outer", "link"), None),
            P(),
            P(),
            P(),
            P(),
            P(),
            P(),
            P(),
        ),
        out_specs=(
            P("replica", ("outer", "link"), None),
            P("replica", ("outer", "link"), None),
            P("replica", ("outer", "link"), None),
            P("replica", ("outer", "link"), None),
            P(),
            P(),
            P(),
            P(),
            P(),
            P(),
            P(),
        ),
        check_vma=False,
    )
```

```python
import functools

import jax
import jax.numpy as jnp
from jax import lax
from jax.experimental import pallas as pl
from jax.experimental.pallas import tpu as pltpu
from jax.sharding import PartitionSpec as P

VMEM_BYTES = 56 * 1024 * 1024
MESH = pl.DeviceIdType.MESH
LANES = 128


def mm(a, b):
    return jnp.dot(a, b, preferred_element_type=jnp.float32)


def mm_nt(a, b):
    return lax.dot_general(a, b, (((1,), (1,)), ((), ())), preferred_element_type=jnp.float32)


def mm_tn(a, b):
    return lax.dot_general(a, b, (((0,), (0,)), ((), ())), preferred_element_type=jnp.float32)


def sigmoid(v):
    return 0.5 * jnp.tanh(0.5 * v) + 0.5


def one_hot_rows(col, width):
    ids = lax.broadcasted_iota(jnp.int32, (col.shape[0], width), 1)
    return jnp.where(ids == col, 1.0, 0.0).astype(jnp.bfloat16)


def one_hot_cols(row, height):
    ids = lax.broadcasted_iota(jnp.int32, (height, row.shape[1]), 0)
    return jnp.where(ids == row, 1.0, 0.0).astype(jnp.bfloat16)


def whole(memory_space=pltpu.VMEM):
    return pl.BlockSpec(memory_space=memory_space)


def group_place():
    span = lax.axis_size("link")
    size = lax.axis_size("outer") * span
    return lax.axis_index("outer") * span + lax.axis_index("link"), size, span


def greet(axes):
    barrier = pltpu.get_barrier_semaphore()
    me, size, span = group_place()
    count = size - 1
    for k in range(1, size):
        peer = lax.rem(me + k, size)
        where = {"outer": lax.div(peer, span), "link": lax.rem(peer, span)}
        pl.semaphore_signal(barrier, inc=1, device_id=where, device_id_type=MESH)
    for axis in axes:
        n = lax.axis_size(axis)
        count += n - 1
        for k in range(1, n):
            where = {axis: lax.rem(lax.axis_index(axis) + k, n)}
            pl.semaphore_signal(barrier, inc=1, device_id=where, device_id_type=MESH)
    return barrier, count


def start_exchange(src, dst, send_sem, recv_sem):
    me, size, span = group_place()
    cap = src.shape[0] // size
    mine = pl.ds(pl.multiple_of(me * cap, cap), cap)
    copies = []
    for k in range(1, size):
        peer = lax.rem(me + k, size)
        copy = pltpu.make_async_remote_copy(
            src_ref=src.at[pl.ds(pl.multiple_of(peer * cap, cap), cap)],
            dst_ref=dst.at[mine],
            send_sem=send_sem.at[k - 1],
            recv_sem=recv_sem.at[k - 1],
            device_id={"outer": lax.div(peer, span), "link": lax.rem(peer, span)},
            device_id_type=MESH,
        )
        copy.start()
        copies.append(copy)
    dst[mine, :] = src[mine, :]
    return copies


def serve_kernel(col_ref, link_ref, out_ref, served, send_sem, recv_sem):
    barrier, count = greet(())
    hot = one_hot_rows(col_ref[...], link_ref.shape[0])
    served[...] = mm(hot, link_ref[...]).astype(jnp.bfloat16)
    pl.semaphore_wait(barrier, count)
    for copy in start_exchange(served, out_ref, send_sem, recv_sem):
        copy.wait()


def forward_kernel(
    steps,
    fetched_ref,
    path_ref,
    col_ref,
    row_ref,
    lens_ref,
    wx_ref,
    wh_ref,
    bias_ref,
    xs_ref,
    hs_ref,
    coef_ref,
    partial_ref,
    path_out_ref,
    state,
    total,
    from_input,
    reached,
):
    block = pl.program_id(0)
    flows, width = path_ref.shape
    slots = fetched_ref.shape[0]

    @pl.when(block == 0)
    def _():
        state[...] = path_ref[...].astype(jnp.float32)
        total[...] = jnp.zeros_like(total)

    x = mm(one_hot_rows(col_ref[...], slots), fetched_ref[...]).astype(jnp.bfloat16)
    xs_ref[...] = x
    from_input[...] = mm(x, wx_ref[...]) + bias_ref[...]
    h = state[...]
    for u in range(steps):
        rows = pl.ds(u * flows, flows)
        live = lens_ref[...] > block * steps + u
        h_bf = h.astype(jnp.bfloat16)
        hs_ref[rows, :] = h_bf
        gs = mm(h_bf, wh_ref[...])
        gi = from_input[rows, :]
        z = sigmoid(gi[:, :width] + gs[:, :width])
        r = sigmoid(gi[:, width : 2 * width] + gs[:, width : 2 * width])
        gs3 = gs[:, 2 * width :]
        n = jnp.tanh(gi[:, 2 * width :] + r * gs3)
        diff = h - n
        h = jnp.where(live, n + z * diff, h)
        reached[rows, :] = jnp.where(live, h, 0.0).astype(jnp.bfloat16)
        rest = 1.0 - z
        c_n = jnp.where(live, rest * (1.0 - n * n), 0.0)
        coef_ref[rows, :width] = jnp.where(live, diff * z * rest, 0.0)
        coef_ref[rows, width : 2 * width] = c_n * gs3 * r * (1.0 - r)
        coef_ref[rows, 2 * width : 3 * width] = c_n
        coef_ref[rows, 3 * width : 4 * width] = c_n * r
        coef_ref[rows, 4 * width :] = jnp.where(live, z, 1.0)
    state[...] = h
    total[...] += mm(one_hot_cols(row_ref[0], slots), reached[...])

    @pl.when(block == pl.num_programs(0) - 1)
    def _():
        partial_ref[...] = total[...].astype(jnp.bfloat16)
        path_out_ref[...] = state[...].astype(jnp.bfloat16)


def link_kernel(
    partial_ref,
    row_ref,
    col_ref,
    link_ref,
    grad_ref,
    keep_ref,
    w1_ref,
    b1_ref,
    w2_ref,
    b2_ref,
    link_out_ref,
    direct_ref,
    returned_ref,
    grad_w_ref,
    grad_b_ref,
    arrived,
    back,
    send_sem,
    recv_sem,
):
    barrier, count = greet(())
    pl.semaphore_wait(barrier, count)
    incoming = start_exchange(partial_ref, arrived, send_sem.at[0], recv_sem.at[0])
    links, width = link_ref.shape
    rows = link_ref[...]
    keep = keep_ref[...]
    gv = keep * grad_ref[...].astype(jnp.float32)
    gv_bf = gv.astype(jnp.bfloat16)
    d_act = mm_nt(gv_bf, w2_ref[...])
    u = mm(rows, w1_ref[:width, :]) + b1_ref[...]
    for copy in incoming:
        copy.wait()
    agg = mm(one_hot_cols(row_ref[...], links), arrived[...]).astype(jnp.bfloat16)
    u = u + mm(agg, w1_ref[width:, :])
    s = sigmoid(u)
    du = d_act * s * (1.0 + u * (1.0 - s))
    du_bf = du.astype(jnp.bfloat16)
    d_agg = mm_nt(du_bf, w1_ref[width:, :]).astype(jnp.bfloat16)
    back[...] = mm(one_hot_rows(col_ref[...], links), d_agg).astype(jnp.bfloat16)
    outgoing = start_exchange(back, returned_ref, send_sem.at[1], recv_sem.at[1])
    act = (u * s).astype(jnp.bfloat16)
    value = rows.astype(jnp.float32) + mm(act, w2_ref[...]) + b2_ref[...]
    link_out_ref[...] = (keep * value).astype(jnp.bfloat16)
    direct_ref[...] = gv + mm_nt(du_bf, w1_ref[:width, :])
    grads = (mm_tn(rows, du_bf), mm_tn(agg, du_bf), mm_tn(act, gv_bf))
    for k, grad in enumerate(grads):
        put_lanes(grad_w_ref, grad, 3 * width, k * width)
    grad_b_ref[...] = jnp.zeros_like(grad_b_ref)
    for k, term in enumerate((du, gv)):
        put_lanes(grad_b_ref, jnp.sum(term, axis=0, keepdims=True), 1, k * (width // LANES))
    for copy in outgoing:
        copy.wait()


def put_lanes(out_ref, value, pitch, first):
    for k in range(value.shape[1] // LANES):
        piece = value[:, k * LANES : (k + 1) * LANES].astype(out_ref.dtype)
        out_ref[pl.ds(k * pitch + first, value.shape[0]), :] = piece


def get_lanes(ref, part, pitch, first, count, width):
    pieces = [
        ref[part, pl.ds(k * pitch + first, count), :].astype(jnp.float32)
        for k in range(width // LANES)
    ]
    return jnp.concatenate(pieces, axis=1)


ORDERS = (
    ("outer", "replica", "link"),
    ("replica", "outer", "link"),
    ("replica", "outer", "link"),
)


def reduce_layout(rows, order):
    places, size, offset = [], rows, 0
    for axis in order:
        n = lax.axis_size(axis)
        size = size // n
        places.append((axis, n, size, offset))
        offset = offset + lax.axis_index(axis) * size
    return places


def send_all(axis, n, source, target, send_sem, recv_sem):
    copies = []
    for k in range(1, n):
        peer = lax.rem(lax.axis_index(axis) + k, n)
        copy = pltpu.make_async_remote_copy(
            src_ref=source(peer),
            dst_ref=target(k - 1),
            send_sem=send_sem.at[k - 1],
            recv_sem=recv_sem.at[k - 1],
            device_id={axis: peer},
            device_id_type=MESH,
        )
        copy.start()
        copies.append(copy)
    return copies


def tail_kernel(
    dpart_ref,
    first_ref,
    second_ref,
    third_ref,
    bias_a_ref,
    bias_b_ref,
    owned_ref,
    sums_ref,
    bias_ref,
    *scratch,
):
    landing = scratch[:9]
    held = scratch[9:15]
    bias_now, bias_in, send_sem, recv_sem, swap_send, swap_recv = scratch[15:]
    barrier, count = greet(("replica", "outer", "link"))
    bias_now[0, :8, :] = bias_a_ref[...]
    bias_now[0, 8:, :] = bias_b_ref[...]
    pl.semaphore_wait(barrier, count)
    inputs = (first_ref, second_ref, third_ref)
    rows = first_ref.shape[0]
    layouts = [reduce_layout(rows, order) for order in ORDERS]
    swaps = []
    for phase in range(3):
        started = []
        for part in range(3):
            axis, n, size, _ = layouts[part][phase]
            now = inputs[part] if phase == 0 else held[part * 2 + phase - 1]
            land = landing[part * 3 + phase]

            def source(peer, now=now, size=size):
                return now.at[pl.ds(pl.multiple_of(peer * size, 16), size)]

            started.append(
                send_all(
                    axis,
                    n,
                    source,
                    lambda k, land=land: land.at[k],
                    send_sem.at[part, phase],
                    recv_sem.at[part, phase],
                )
            )
        axis, n = layouts[0][phase][:2]
        started.append(
            send_all(
                axis,
                n,
                lambda peer, phase=phase: bias_now.at[phase],
                lambda k, phase=phase: bias_in.at[phase, k],
                send_sem.at[3, phase],
                recv_sem.at[3, phase],
            )
        )
        if phase == 0:
            swaps = start_exchange(dpart_ref, owned_ref, swap_send, swap_recv)
        for part in range(3):
            axis, n, size, offset = layouts[part][phase]
            now = inputs[part] if phase == 0 else held[part * 2 + phase - 1]
            land = landing[part * 3 + phase]
            for copy in started[part]:
                copy.wait()
            place = lax.axis_index(axis)
            mine = now[pl.ds(pl.multiple_of(place * size, 16), size), :].astype(jnp.float32)
            for k in range(n - 1):
                mine = mine + land[k].astype(jnp.float32)
            mine = mine.astype(jnp.bfloat16)
            if phase < 2:
                held[part * 2 + phase][...] = mine
            else:
                sums_ref[part, pl.ds(pl.multiple_of(offset + place * size, 16), size), :] = mine
        for copy in started[3]:
            copy.wait()
        total = bias_now[phase]
        for k in range(n_of(layouts[0][phase]) - 1):
            total = total + bias_in[phase, k]
        if phase < 2:
            bias_now[phase + 1] = total
        else:
            bias_ref[...] = total
    for phase in (2, 1, 0):
        started = []
        for part in range(3):
            axis, n, size, offset = layouts[part][phase]
            start = pl.multiple_of(offset + lax.axis_index(axis) * size, 16)
            region = sums_ref.at[part, pl.ds(start, size)]
            started += send_all(
                axis,
                n,
                lambda peer, region=region: region,
                lambda k, region=region: region,
                send_sem.at[part, 3 + phase],
                recv_sem.at[part, 3 + phase],
            )
        for copy in started:
            copy.wait()
    for copy in swaps:
        copy.wait()


def n_of(place):
    return place[1]


def backward_kernel(
    steps,
    returned_ref,
    path_grad_ref,
    col_ref,
    row_ref,
    lens_ref,
    wx_ref,
    wh_ref,
    xs_ref,
    hs_ref,
    coef_ref,
    dpart_ref,
    path_back_ref,
    grad_wx_ref,
    grad_wh_ref,
    grad_b_ref,
    carry,
    total,
    hop_grad,
    dgi,
    dgs,
    acc_wx,
    acc_wh,
    acc_b,
):
    block = pl.num_programs(0) - 1 - pl.program_id(0)
    flows, width = path_grad_ref.shape
    slots = returned_ref.shape[0]

    @pl.when(pl.program_id(0) == 0)
    def _():
        carry[...] = path_grad_ref[...].astype(jnp.float32)
        total[...] = jnp.zeros_like(total)
        acc_wx[...] = jnp.zeros_like(acc_wx)
        acc_wh[...] = jnp.zeros_like(acc_wh)
        acc_b[...] = jnp.zeros_like(acc_b)

    hop_grad[...] = mm(one_hot_rows(col_ref[...], slots), returned_ref[...])
    g = carry[...]
    for u in reversed(range(steps)):
        rows = pl.ds(u * flows, flows)
        live = lens_ref[...] > block * steps + u
        g = g + jnp.where(live, hop_grad[rows, :], 0.0)
        a_z = g * coef_ref[rows, :width]
        a_r = g * coef_ref[rows, width : 2 * width]
        a_n = g * coef_ref[rows, 2 * width : 3 * width]
        a_h = g * coef_ref[rows, 3 * width : 4 * width]
        z_bf = a_z.astype(jnp.bfloat16)
        r_bf = a_r.astype(jnp.bfloat16)
        dgs[rows, :width] = z_bf
        dgs[rows, width : 2 * width] = r_bf
        dgs[rows, 2 * width :] = a_h.astype(jnp.bfloat16)
        g = g * coef_ref[rows, 4 * width :] + mm_nt(dgs[rows, :], wh_ref[...])
        dgi[rows, :width] = z_bf
        dgi[rows, width : 2 * width] = r_bf
        dgi[rows, 2 * width :] = a_n.astype(jnp.bfloat16)
        for k, a in enumerate((a_z, a_r, a_n)):
            folded = jnp.sum(a.reshape(flows // 8, 8, width), axis=0)
            acc_b[:, k * width : (k + 1) * width] += folded
    carry[...] = g
    dx = mm_nt(dgi[...], wx_ref[...]).astype(jnp.bfloat16)
    total[...] += mm(one_hot_cols(row_ref[0], slots), dx)
    acc_wx[...] += mm_tn(xs_ref[...], dgi[...])
    acc_wh[...] += mm_tn(hs_ref[...], dgs[...])

    @pl.when(pl.program_id(0) == pl.num_programs(0) - 1)
    def _():
        dpart_ref[...] = total[...].astype(jnp.bfloat16)
        path_back_ref[...] = carry[...]
        emit_grads(acc_wx, acc_wh, acc_b, grad_wx_ref, grad_wh_ref, grad_b_ref)


def collect_kernel(
    scale,
    owned_ref,
    row_ref,
    direct_ref,
    sums_ref,
    bias_ref,
    out_ref,
    wx_ref,
    wh_ref,
    bias_out_ref,
    w1_ref,
    b1_ref,
    w2_ref,
    b2_ref,
):
    width = direct_ref.shape[1]
    hot = one_hot_cols(row_ref[...], direct_ref.shape[0])
    out_ref[...] = direct_ref[...] + mm(hot, owned_ref[...])
    wx_ref[...] = get_lanes(sums_ref, 0, width, 0, width, 3 * width) * scale
    wh_ref[...] = get_lanes(sums_ref, 1, width, 0, width, 3 * width) * scale
    w1_ref[...] = get_lanes(sums_ref, 2, 3 * width, 0, 2 * width, width) * scale
    w2_ref[...] = get_lanes(sums_ref, 2, 3 * width, 2 * width, width, width) * scale
    bias = bias_ref[...] * scale
    for k in range(3 * width // LANES):
        bias_out_ref[:, k * LANES : (k + 1) * LANES] = bias[k : k + 1, :]
    for k in range(width // LANES):
        lanes = slice(k * LANES, (k + 1) * LANES)
        b1_ref[:, lanes] = bias[8 + k : 9 + k, :]
        b2_ref[:, lanes] = bias[8 + width // LANES + k : 9 + width // LANES + k, :]


def call(kernel, out_shapes, collective_id=None, **options):
    return pl.pallas_call(
        kernel,
        out_shape=[jax.ShapeDtypeStruct(shape, dtype) for shape, dtype in out_shapes],
        compiler_params=pltpu.CompilerParams(
            vmem_limit_bytes=VMEM_BYTES,
            collective_id=collective_id,
            has_side_effects=collective_id is not None,
        ),
        **options,
    )


def emit_grads(acc_wx, acc_wh, acc_b, grad_wx_ref, grad_wh_ref, grad_b_ref):
    width = acc_wx.shape[0]
    put_lanes(grad_wx_ref, acc_wx[...], width, 0)
    put_lanes(grad_wh_ref, acc_wh[...], width, 0)
    grad_b_ref[...] = jnp.zeros_like(grad_b_ref)
    put_lanes(grad_b_ref, jnp.sum(acc_b[...], axis=0, keepdims=True), 1, 0)


def grad_shapes(slots, flows, width):
    rows = 3 * width * width // LANES
    return [
        ((slots, width), jnp.bfloat16),
        ((flows, width), jnp.float32),
        ((rows, LANES), jnp.bfloat16),
        ((rows, LANES), jnp.bfloat16),
        ((8, LANES), jnp.float32),
    ]


def tail_scratch(rows):
    bf, f32 = jnp.bfloat16, jnp.float32
    landing, held = [], []
    for order in ORDERS:
        size = rows
        for phase, axis in enumerate(order):
            n = lax.axis_size(axis)
            size = size // n
            landing.append(pltpu.VMEM((n - 1, size, LANES), bf))
            if phase < 2:
                held.append(pltpu.VMEM((size, LANES), bf))
    most = max(lax.axis_size(axis) for axis in ORDERS[0]) - 1
    peers = lax.axis_size("outer") * lax.axis_size("link") - 1
    return landing + held + [
        pltpu.VMEM((3, 16, LANES), f32),
        pltpu.VMEM((3, most, 16, LANES), f32),
        pltpu.SemaphoreType.DMA((4, 6, most)),
        pltpu.SemaphoreType.DMA((4, 6, most)),
        pltpu.SemaphoreType.DMA((peers,)),
        pltpu.SemaphoreType.DMA((peers,)),
    ]


def body(
    link_in,
    path_in,
    hop_slots,
    hop_lens,
    failed,
    serve_index,
    link_grad,
    path_grad,
    gru_wx,
    gru_wh,
    gru_bias,
    mlp_w1,
    mlp_b1,
    mlp_w2,
    mlp_b2,
):
    bf, f32 = jnp.bfloat16, jnp.float32
    link_rows = link_in[0]
    links, width = link_rows.shape
    serve_rows = serve_index[0, :, 0, :]
    group, cap = serve_rows.shape
    slots = group * cap
    serve_row = serve_rows.reshape(1, slots)
    serve_col = serve_rows.reshape(slots, 1)
    flows, hops = hop_slots.shape[1:]
    steps = 4 if hops % 4 == 0 else 1
    blocks = hops // steps
    slot_ids = hop_slots[0].T
    slot_col = slot_ids.reshape(hops * flows, 1)
    slot_row = slot_ids.reshape(blocks, 1, steps * flows)
    lens_col = hop_lens[0].reshape(flows, 1)
    keep_col = (1 - failed[0]).astype(f32)[:, None]
    span = steps * flows

    peers = group - 1
    fetched = call(
        serve_kernel,
        [((slots, width), bf)],
        collective_id=0,
        in_specs=[whole()] * 2,
        out_specs=[whole()],
        scratch_shapes=[
            pltpu.VMEM((slots, width), bf),
            pltpu.SemaphoreType.DMA((peers,)),
            pltpu.SemaphoreType.DMA((peers,)),
        ],
    )(serve_col, link_rows)[0]

    def fixed(*shape):
        return pl.BlockSpec(shape, lambda i: (0,) * len(shape))

    def ahead(*shape):
        return pl.BlockSpec(shape, lambda i: (i,) + (0,) * (len(shape) - 1))

    def behind(*shape):
        return pl.BlockSpec(shape, lambda i: (blocks - 1 - i,) + (0,) * (len(shape) - 1))

    xs, hs, coef, partial_value, path_out = call(
        functools.partial(forward_kernel, steps),
        [
            ((hops * flows, width), bf),
            ((hops * flows, width), bf),
            ((hops * flows, 5 * width), f32),
            ((slots, width), bf),
            ((flows, width), bf),
        ],
        grid=(blocks,),
        in_specs=[
            fixed(slots, width),
            fixed(flows, width),
            ahead(span, 1),
            ahead(1, 1, span),
            fixed(flows, 1),
            fixed(width, 3 * width),
            fixed(width, 3 * width),
            fixed(1, 3 * width),
        ],
        out_specs=[
            ahead(span, width),
            ahead(span, width),
            ahead(span, 5 * width),
            fixed(slots, width),
            fixed(flows, width),
        ],
        scratch_shapes=[
            pltpu.VMEM((flows, width), f32),
            pltpu.VMEM((slots, width), f32),
            pltpu.VMEM((span, 3 * width), f32),
            pltpu.VMEM((span, width), bf),
        ],
    )(fetched, path_in[0], slot_col, slot_row, lens_col, gru_wx, gru_wh, gru_bias[None])
    link_out, direct, returned, grad_w, grad_b = call(
        link_kernel,
        [
            ((links, width), bf),
            ((links, width), f32),
            ((slots, width), bf),
            ((3 * width * width // LANES, LANES), bf),
            ((8, LANES), f32),
        ],
        collective_id=1,
        in_specs=[whole()] * 10,
        out_specs=[whole()] * 5,
        scratch_shapes=[
            pltpu.VMEM((slots, width), bf),
            pltpu.VMEM((slots, width), bf),
            pltpu.SemaphoreType.DMA((2, peers)),
            pltpu.SemaphoreType.DMA((2, peers)),
        ],
    )(
        partial_value,
        serve_row,
        serve_col,
        link_rows,
        link_grad[0],
        keep_col,
        mlp_w1,
        mlp_b1[None],
        mlp_w2,
        mlp_b2[None],
    )
    dpart, path_back, grad_wx, grad_wh, grad_bias = call(
        functools.partial(backward_kernel, steps),
        grad_shapes(slots, flows, width),
        grid=(blocks,),
        in_specs=[
            fixed(slots, width),
            fixed(flows, width),
            behind(span, 1),
            behind(1, 1, span),
            fixed(flows, 1),
            fixed(width, 3 * width),
            fixed(width, 3 * width),
            behind(span, width),
            behind(span, width),
            behind(span, 5 * width),
        ],
        out_specs=[fixed(*shape) for shape, _ in grad_shapes(slots, flows, width)],
        scratch_shapes=[
            pltpu.VMEM((flows, width), f32),
            pltpu.VMEM((slots, width), f32),
            pltpu.VMEM((span, width), f32),
            pltpu.VMEM((span, 3 * width), bf),
            pltpu.VMEM((span, 3 * width), bf),
            pltpu.VMEM((width, 3 * width), f32),
            pltpu.VMEM((width, 3 * width), f32),
            pltpu.VMEM((8, 3 * width), f32),
        ],
    )(
        returned,
        path_grad[0],
        slot_col,
        slot_row,
        lens_col,
        gru_wx,
        gru_wh,
        xs,
        hs,
        coef,
    )
    devices = lax.axis_size("replica") * lax.axis_size("outer") * lax.axis_size("link")
    scale = float(devices * links) ** (-0.5)
    rows = grad_w.shape[0]
    padded = -(-rows // (16 * devices)) * 16 * devices
    grads = [grad_wx, grad_wh, grad_w]
    if padded != rows:
        grads = [jnp.pad(grad, ((0, padded - rows), (0, 0))) for grad in grads]
    owned, sums, biases = call(
        tail_kernel,
        [((slots, width), bf), ((3, padded, LANES), bf), ((16, LANES), f32)],
        collective_id=2,
        in_specs=[whole()] * 6,
        out_specs=[whole()] * 3,
        scratch_shapes=tail_scratch(padded),
    )(dpart, *grads, grad_bias, grad_b)
    link_back, total_wx, total_wh, total_b, total_w1, total_b1, total_w2, total_b2 = call(
        functools.partial(collect_kernel, scale),
        [
            ((links, width), f32),
            ((width, 3 * width), f32),
            ((width, 3 * width), f32),
            ((1, 3 * width), f32),
            ((2 * width, width), f32),
            ((1, width), f32),
            ((width, width), f32),
            ((1, width), f32),
        ],
        in_specs=[whole()] * 5,
        out_specs=[whole()] * 8,
    )(owned, serve_row, direct, sums, biases)
    return (
        link_out[None],
        path_out[None],
        link_back[None],
        path_back[None],
        total_wx,
        total_wh,
        total_b[0],
        total_w1,
        total_b1[0],
        total_w2,
        total_b2[0],
    )


def solution(mesh):
    return jax.shard_map(
        body,
        mesh=mesh,
        in_specs=(
            P("replica", ("outer", "link"), None),
            P("replica", ("outer", "link"), None),
            P("replica", ("outer", "link"), None),
            P("replica", ("outer", "link")),
            P("replica", ("outer", "link")),
            P("replica", None, ("outer", "link"), None),
            P("replica", ("outer", "link"), None),
            P("replica", ("outer", "link"), None),
            P(),
            P(),
            P(),
            P(),
            P(),
            P(),
            P(),
        ),
        out_specs=(
            P("replica", ("outer", "link"), None),
            P("replica", ("outer", "link"), None),
            P("replica", ("outer", "link"), None),
            P("replica", ("outer", "link"), None),
            P(),
            P(),
            P(),
            P(),
            P(),
            P(),
            P(),
        ),
        check_vma=False,
    )
```

```python
import functools

import jax
import jax.numpy as jnp
from jax import lax
from jax.experimental import pallas as pl
from jax.experimental.pallas import tpu as pltpu
from jax.sharding import PartitionSpec as P

VMEM_BYTES = 56 * 1024 * 1024
MESH = pl.DeviceIdType.MESH
LANES = 128


def mm(a, b):
    return jnp.dot(a, b, preferred_element_type=jnp.float32)


def mm_nt(a, b):
    return lax.dot_general(a, b, (((1,), (1,)), ((), ())), preferred_element_type=jnp.float32)


def mm_tn(a, b):
    return lax.dot_general(a, b, (((0,), (0,)), ((), ())), preferred_element_type=jnp.float32)


def sigmoid(v):
    return 0.5 * jnp.tanh(0.5 * v) + 0.5


def one_hot_rows(col, width):
    ids = lax.broadcasted_iota(jnp.int32, (col.shape[0], width), 1)
    return jnp.where(ids == col, 1.0, 0.0).astype(jnp.bfloat16)


def one_hot_cols(row, height):
    ids = lax.broadcasted_iota(jnp.int32, (height, row.shape[1]), 0)
    return jnp.where(ids == row, 1.0, 0.0).astype(jnp.bfloat16)


def whole(memory_space=pltpu.VMEM):
    return pl.BlockSpec(memory_space=memory_space)


def group_place():
    span = lax.axis_size("link")
    size = lax.axis_size("outer") * span
    return lax.axis_index("outer") * span + lax.axis_index("link"), size, span


def greet(axes):
    barrier = pltpu.get_barrier_semaphore()
    me, size, span = group_place()
    count = size - 1
    for k in range(1, size):
        peer = lax.rem(me + k, size)
        where = {"outer": lax.div(peer, span), "link": lax.rem(peer, span)}
        pl.semaphore_signal(barrier, inc=1, device_id=where, device_id_type=MESH)
    for axis in axes:
        n = lax.axis_size(axis)
        count += n - 1
        for k in range(1, n):
            where = {axis: lax.rem(lax.axis_index(axis) + k, n)}
            pl.semaphore_signal(barrier, inc=1, device_id=where, device_id_type=MESH)
    return barrier, count


def start_exchange(src, dst, send_sem, recv_sem):
    me, size, span = group_place()
    cap = src.shape[0] // size
    mine = pl.ds(pl.multiple_of(me * cap, cap), cap)
    copies = []
    for k in range(1, size):
        peer = lax.rem(me + k, size)
        copy = pltpu.make_async_remote_copy(
            src_ref=src.at[pl.ds(pl.multiple_of(peer * cap, cap), cap)],
            dst_ref=dst.at[mine],
            send_sem=send_sem.at[k - 1],
            recv_sem=recv_sem.at[k - 1],
            device_id={"outer": lax.div(peer, span), "link": lax.rem(peer, span)},
            device_id_type=MESH,
        )
        copy.start()
        copies.append(copy)
    dst[mine, :] = src[mine, :]
    return copies


def serve_kernel(col_ref, link_ref, out_ref, served, send_sem, recv_sem):
    barrier, count = greet(())
    hot = one_hot_rows(col_ref[...], link_ref.shape[0])
    served[...] = mm(hot, link_ref[...]).astype(jnp.bfloat16)
    pl.semaphore_wait(barrier, count)
    for copy in start_exchange(served, out_ref, send_sem, recv_sem):
        copy.wait()


def forward_kernel(
    steps,
    fetched_ref,
    path_ref,
    col_ref,
    row_ref,
    lens_ref,
    wx_ref,
    wh_ref,
    bias_ref,
    xs_ref,
    hs_ref,
    coef_ref,
    partial_ref,
    path_out_ref,
    state,
    total,
    from_input,
    reached,
):
    block = pl.program_id(0)
    flows, width = path_ref.shape
    slots = fetched_ref.shape[0]

    @pl.when(block == 0)
    def _():
        state[...] = path_ref[...].astype(jnp.float32)
        total[...] = jnp.zeros_like(total)

    x = mm(one_hot_rows(col_ref[...], slots), fetched_ref[...]).astype(jnp.bfloat16)
    xs_ref[...] = x
    from_input[...] = mm(x, wx_ref[...]) + bias_ref[...]
    h = state[...]
    for u in range(steps):
        rows = pl.ds(u * flows, flows)
        live = lens_ref[...] > block * steps + u
        h_bf = h.astype(jnp.bfloat16)
        hs_ref[rows, :] = h_bf
        gs = mm(h_bf, wh_ref[...])
        gi = from_input[rows, :]
        z = sigmoid(gi[:, :width] + gs[:, :width])
        r = sigmoid(gi[:, width : 2 * width] + gs[:, width : 2 * width])
        gs3 = gs[:, 2 * width :]
        n = jnp.tanh(gi[:, 2 * width :] + r * gs3)
        diff = h - n
        h = jnp.where(live, n + z * diff, h)
        reached[rows, :] = jnp.where(live, h, 0.0).astype(jnp.bfloat16)
        rest = 1.0 - z
        c_n = jnp.where(live, rest * (1.0 - n * n), 0.0)
        coef_ref[rows, :width] = jnp.where(live, diff * z * rest, 0.0)
        coef_ref[rows, width : 2 * width] = c_n * gs3 * r * (1.0 - r)
        coef_ref[rows, 2 * width : 3 * width] = c_n
        coef_ref[rows, 3 * width : 4 * width] = c_n * r
        coef_ref[rows, 4 * width :] = jnp.where(live, z, 1.0)
    state[...] = h
    total[...] += mm(one_hot_cols(row_ref[0], slots), reached[...])

    @pl.when(block == pl.num_programs(0) - 1)
    def _():
        partial_ref[...] = total[...].astype(jnp.bfloat16)
        path_out_ref[...] = state[...].astype(jnp.bfloat16)


def link_kernel(
    partial_ref,
    row_ref,
    col_ref,
    link_ref,
    grad_ref,
    keep_ref,
    w1_ref,
    b1_ref,
    w2_ref,
    b2_ref,
    link_out_ref,
    direct_ref,
    returned_ref,
    grad_w_ref,
    grad_b_ref,
    arrived,
    back,
    send_sem,
    recv_sem,
):
    barrier, count = greet(())
    pl.semaphore_wait(barrier, count)
    incoming = start_exchange(partial_ref, arrived, send_sem.at[0], recv_sem.at[0])
    links, width = link_ref.shape
    rows = link_ref[...]
    keep = keep_ref[...]
    gv = keep * grad_ref[...].astype(jnp.float32)
    gv_bf = gv.astype(jnp.bfloat16)
    d_act = mm_nt(gv_bf, w2_ref[...])
    u = mm(rows, w1_ref[:width, :]) + b1_ref[...]
    for copy in incoming:
        copy.wait()
    agg = mm(one_hot_cols(row_ref[...], links), arrived[...]).astype(jnp.bfloat16)
    u = u + mm(agg, w1_ref[width:, :])
    s = sigmoid(u)
    du = d_act * s * (1.0 + u * (1.0 - s))
    du_bf = du.astype(jnp.bfloat16)
    d_agg = mm_nt(du_bf, w1_ref[width:, :]).astype(jnp.bfloat16)
    back[...] = mm(one_hot_rows(col_ref[...], links), d_agg).astype(jnp.bfloat16)
    outgoing = start_exchange(back, returned_ref, send_sem.at[1], recv_sem.at[1])
    act = (u * s).astype(jnp.bfloat16)
    value = rows.astype(jnp.float32) + mm(act, w2_ref[...]) + b2_ref[...]
    link_out_ref[...] = (keep * value).astype(jnp.bfloat16)
    direct_ref[...] = gv + mm_nt(du_bf, w1_ref[:width, :])
    grads = (mm_tn(rows, du_bf), mm_tn(agg, du_bf), mm_tn(act, gv_bf))
    for k, grad in enumerate(grads):
        put_lanes(grad_w_ref, grad, 3 * width, k * width)
    grad_b_ref[...] = jnp.zeros_like(grad_b_ref)
    for k, term in enumerate((du, gv)):
        put_lanes(grad_b_ref, jnp.sum(term, axis=0, keepdims=True), 1, k * (width // LANES))
    for copy in outgoing:
        copy.wait()


def put_lanes(out_ref, value, pitch, first):
    for k in range(value.shape[1] // LANES):
        piece = value[:, k * LANES : (k + 1) * LANES].astype(out_ref.dtype)
        out_ref[pl.ds(k * pitch + first, value.shape[0]), :] = piece


def get_lanes(ref, part, pitch, first, count, width):
    pieces = [
        ref[part, pl.ds(k * pitch + first, count), :].astype(jnp.float32)
        for k in range(width // LANES)
    ]
    return jnp.concatenate(pieces, axis=1)


ORDERS = (
    ("outer", "replica", "link"),
    ("replica", "outer", "link"),
    ("replica", "outer", "link"),
)


def reduce_layout(rows, order):
    places, size, offset = [], rows, 0
    for axis in order:
        n = lax.axis_size(axis)
        size = size // n
        places.append((axis, n, size, offset))
        offset = offset + lax.axis_index(axis) * size
    return places


def send_all(axis, n, source, target, send_sem, recv_sem):
    copies = []
    for k in range(1, n):
        peer = lax.rem(lax.axis_index(axis) + k, n)
        copy = pltpu.make_async_remote_copy(
            src_ref=source(peer),
            dst_ref=target(k - 1),
            send_sem=send_sem.at[k - 1],
            recv_sem=recv_sem.at[k - 1],
            device_id={axis: peer},
            device_id_type=MESH,
        )
        copy.start()
        copies.append(copy)
    return copies


def tail_kernel(
    dpart_ref,
    first_ref,
    second_ref,
    third_ref,
    bias_a_ref,
    bias_b_ref,
    owned_ref,
    sums_ref,
    bias_ref,
    *scratch,
):
    landing = scratch[:9]
    held = scratch[9:15]
    bias_now, bias_in, send_sem, recv_sem, swap_send, swap_recv = scratch[15:]
    barrier, count = greet(("replica", "outer", "link"))
    bias_now[0, :8, :] = bias_a_ref[...]
    bias_now[0, 8:, :] = bias_b_ref[...]
    pl.semaphore_wait(barrier, count)
    inputs = (first_ref, second_ref, third_ref)
    rows = first_ref.shape[0]
    layouts = [reduce_layout(rows, order) for order in ORDERS]

    def begin(part, stage):
        if stage < 3:
            axis, n, size, _ = layouts[part][stage]
            now = inputs[part] if stage == 0 else held[part * 2 + stage - 1]
            land = landing[part * 3 + stage]

            def source(peer):
                return now.at[pl.ds(pl.multiple_of(peer * size, 16), size)]

            def target(k):
                return land.at[k]

        else:
            axis, n, size, offset = layouts[part][5 - stage]
            start = pl.multiple_of(offset + lax.axis_index(axis) * size, 16)

            def source(peer):
                return sums_ref.at[part, pl.ds(start, size)]

            def target(k):
                return sums_ref.at[part, pl.ds(start, size)]

        return send_all(
            axis, n, source, target, send_sem.at[part, stage], recv_sem.at[part, stage]
        )

    def begin_bias(phase):
        axis, n = layouts[0][phase][:2]
        return send_all(
            axis,
            n,
            lambda peer: bias_now.at[phase],
            lambda k: bias_in.at[phase, k],
            send_sem.at[3, phase],
            recv_sem.at[3, phase],
        )

    def add_up(part, phase):
        axis, n, size, offset = layouts[part][phase]
        now = inputs[part] if phase == 0 else held[part * 2 + phase - 1]
        land = landing[part * 3 + phase]
        place = lax.axis_index(axis)
        mine = now[pl.ds(pl.multiple_of(place * size, 16), size), :].astype(jnp.float32)
        for k in range(n - 1):
            mine = mine + land[k].astype(jnp.float32)
        mine = mine.astype(jnp.bfloat16)
        if phase < 2:
            held[part * 2 + phase][...] = mine
        else:
            sums_ref[part, pl.ds(pl.multiple_of(offset + place * size, 16), size), :] = mine

    started = [begin(part, 0) for part in range(3)]
    bias_copies = begin_bias(0)
    swaps = start_exchange(dpart_ref, owned_ref, swap_send, swap_recv)
    for stage in range(6):
        for part in range(3):
            for copy in started[part]:
                copy.wait()
            if stage < 3:
                add_up(part, stage)
            if stage < 5:
                started[part] = begin(part, stage + 1)
        if stage < 3:
            for copy in bias_copies:
                copy.wait()
            total = bias_now[stage]
            for k in range(n_of(layouts[0][stage]) - 1):
                total = total + bias_in[stage, k]
            if stage < 2:
                bias_now[stage + 1] = total
                bias_copies = begin_bias(stage + 1)
            else:
                bias_ref[...] = total
    for copy in swaps:
        copy.wait()


def n_of(place):
    return place[1]


def backward_kernel(
    steps,
    returned_ref,
    path_grad_ref,
    col_ref,
    row_ref,
    lens_ref,
    wx_ref,
    wh_ref,
    xs_ref,
    hs_ref,
    coef_ref,
    dpart_ref,
    path_back_ref,
    grad_wx_ref,
    grad_wh_ref,
    grad_b_ref,
    carry,
    total,
    hop_grad,
    dgi,
    dgs,
    acc_wx,
    acc_wh,
    acc_b,
):
    block = pl.num_programs(0) - 1 - pl.program_id(0)
    flows, width = path_grad_ref.shape
    slots = returned_ref.shape[0]

    @pl.when(pl.program_id(0) == 0)
    def _():
        carry[...] = path_grad_ref[...].astype(jnp.float32)
        total[...] = jnp.zeros_like(total)
        acc_wx[...] = jnp.zeros_like(acc_wx)
        acc_wh[...] = jnp.zeros_like(acc_wh)
        acc_b[...] = jnp.zeros_like(acc_b)

    hop_grad[...] = mm(one_hot_rows(col_ref[...], slots), returned_ref[...])
    g = carry[...]
    for u in reversed(range(steps)):
        rows = pl.ds(u * flows, flows)
        live = lens_ref[...] > block * steps + u
        g = g + jnp.where(live, hop_grad[rows, :], 0.0)
        a_z = g * coef_ref[rows, :width]
        a_r = g * coef_ref[rows, width : 2 * width]
        a_n = g * coef_ref[rows, 2 * width : 3 * width]
        a_h = g * coef_ref[rows, 3 * width : 4 * width]
        z_bf = a_z.astype(jnp.bfloat16)
        r_bf = a_r.astype(jnp.bfloat16)
        dgs[rows, :width] = z_bf
        dgs[rows, width : 2 * width] = r_bf
        dgs[rows, 2 * width :] = a_h.astype(jnp.bfloat16)
        g = g * coef_ref[rows, 4 * width :] + mm_nt(dgs[rows, :], wh_ref[...])
        dgi[rows, :width] = z_bf
        dgi[rows, width : 2 * width] = r_bf
        dgi[rows, 2 * width :] = a_n.astype(jnp.bfloat16)
        for k, a in enumerate((a_z, a_r, a_n)):
            folded = jnp.sum(a.reshape(flows // 8, 8, width), axis=0)
            acc_b[:, k * width : (k + 1) * width] += folded
    carry[...] = g
    dx = mm_nt(dgi[...], wx_ref[...]).astype(jnp.bfloat16)
    total[...] += mm(one_hot_cols(row_ref[0], slots), dx)
    acc_wx[...] += mm_tn(xs_ref[...], dgi[...])
    acc_wh[...] += mm_tn(hs_ref[...], dgs[...])

    @pl.when(pl.program_id(0) == pl.num_programs(0) - 1)
    def _():
        dpart_ref[...] = total[...].astype(jnp.bfloat16)
        path_back_ref[...] = carry[...]
        emit_grads(acc_wx, acc_wh, acc_b, grad_wx_ref, grad_wh_ref, grad_b_ref)


def collect_kernel(
    scale,
    owned_ref,
    row_ref,
    direct_ref,
    sums_ref,
    bias_ref,
    out_ref,
    wx_ref,
    wh_ref,
    bias_out_ref,
    w1_ref,
    b1_ref,
    w2_ref,
    b2_ref,
):
    width = direct_ref.shape[1]
    hot = one_hot_cols(row_ref[...], direct_ref.shape[0])
    out_ref[...] = direct_ref[...] + mm(hot, owned_ref[...])
    wx_ref[...] = get_lanes(sums_ref, 0, width, 0, width, 3 * width) * scale
    wh_ref[...] = get_lanes(sums_ref, 1, width, 0, width, 3 * width) * scale
    w1_ref[...] = get_lanes(sums_ref, 2, 3 * width, 0, 2 * width, width) * scale
    w2_ref[...] = get_lanes(sums_ref, 2, 3 * width, 2 * width, width, width) * scale
    bias = bias_ref[...] * scale
    for k in range(3 * width // LANES):
        bias_out_ref[:, k * LANES : (k + 1) * LANES] = bias[k : k + 1, :]
    for k in range(width // LANES):
        lanes = slice(k * LANES, (k + 1) * LANES)
        b1_ref[:, lanes] = bias[8 + k : 9 + k, :]
        b2_ref[:, lanes] = bias[8 + width // LANES + k : 9 + width // LANES + k, :]


def call(kernel, out_shapes, collective_id=None, **options):
    return pl.pallas_call(
        kernel,
        out_shape=[jax.ShapeDtypeStruct(shape, dtype) for shape, dtype in out_shapes],
        compiler_params=pltpu.CompilerParams(
            vmem_limit_bytes=VMEM_BYTES,
            collective_id=collective_id,
            has_side_effects=collective_id is not None,
        ),
        **options,
    )


def emit_grads(acc_wx, acc_wh, acc_b, grad_wx_ref, grad_wh_ref, grad_b_ref):
    width = acc_wx.shape[0]
    put_lanes(grad_wx_ref, acc_wx[...], width, 0)
    put_lanes(grad_wh_ref, acc_wh[...], width, 0)
    grad_b_ref[...] = jnp.zeros_like(grad_b_ref)
    put_lanes(grad_b_ref, jnp.sum(acc_b[...], axis=0, keepdims=True), 1, 0)


def grad_shapes(slots, flows, width):
    rows = 3 * width * width // LANES
    return [
        ((slots, width), jnp.bfloat16),
        ((flows, width), jnp.float32),
        ((rows, LANES), jnp.bfloat16),
        ((rows, LANES), jnp.bfloat16),
        ((8, LANES), jnp.float32),
    ]


def tail_scratch(rows):
    bf, f32 = jnp.bfloat16, jnp.float32
    landing, held = [], []
    for order in ORDERS:
        size = rows
        for phase, axis in enumerate(order):
            n = lax.axis_size(axis)
            size = size // n
            landing.append(pltpu.VMEM((n - 1, size, LANES), bf))
            if phase < 2:
                held.append(pltpu.VMEM((size, LANES), bf))
    most = max(lax.axis_size(axis) for axis in ORDERS[0]) - 1
    peers = lax.axis_size("outer") * lax.axis_size("link") - 1
    return landing + held + [
        pltpu.VMEM((3, 16, LANES), f32),
        pltpu.VMEM((3, most, 16, LANES), f32),
        pltpu.SemaphoreType.DMA((4, 6, most)),
        pltpu.SemaphoreType.DMA((4, 6, most)),
        pltpu.SemaphoreType.DMA((peers,)),
        pltpu.SemaphoreType.DMA((peers,)),
    ]


def body(
    link_in,
    path_in,
    hop_slots,
    hop_lens,
    failed,
    serve_index,
    link_grad,
    path_grad,
    gru_wx,
    gru_wh,
    gru_bias,
    mlp_w1,
    mlp_b1,
    mlp_w2,
    mlp_b2,
):
    bf, f32 = jnp.bfloat16, jnp.float32
    link_rows = link_in[0]
    links, width = link_rows.shape
    serve_rows = serve_index[0, :, 0, :]
    group, cap = serve_rows.shape
    slots = group * cap
    serve_row = serve_rows.reshape(1, slots)
    serve_col = serve_rows.reshape(slots, 1)
    flows, hops = hop_slots.shape[1:]
    steps = 4 if hops % 4 == 0 else 1
    blocks = hops // steps
    slot_ids = hop_slots[0].T
    slot_col = slot_ids.reshape(hops * flows, 1)
    slot_row = slot_ids.reshape(blocks, 1, steps * flows)
    lens_col = hop_lens[0].reshape(flows, 1)
    keep_col = (1 - failed[0]).astype(f32)[:, None]
    span = steps * flows

    peers = group - 1
    fetched = call(
        serve_kernel,
        [((slots, width), bf)],
        collective_id=0,
        in_specs=[whole()] * 2,
        out_specs=[whole()],
        scratch_shapes=[
            pltpu.VMEM((slots, width), bf),
            pltpu.SemaphoreType.DMA((peers,)),
            pltpu.SemaphoreType.DMA((peers,)),
        ],
    )(serve_col, link_rows)[0]

    def fixed(*shape):
        return pl.BlockSpec(shape, lambda i: (0,) * len(shape))

    def ahead(*shape):
        return pl.BlockSpec(shape, lambda i: (i,) + (0,) * (len(shape) - 1))

    def behind(*shape):
        return pl.BlockSpec(shape, lambda i: (blocks - 1 - i,) + (0,) * (len(shape) - 1))

    xs, hs, coef, partial_value, path_out = call(
        functools.partial(forward_kernel, steps),
        [
            ((hops * flows, width), bf),
            ((hops * flows, width), bf),
            ((hops * flows, 5 * width), f32),
            ((slots, width), bf),
            ((flows, width), bf),
        ],
        grid=(blocks,),
        in_specs=[
            fixed(slots, width),
            fixed(flows, width),
            ahead(span, 1),
            ahead(1, 1, span),
            fixed(flows, 1),
            fixed(width, 3 * width),
            fixed(width, 3 * width),
            fixed(1, 3 * width),
        ],
        out_specs=[
            ahead(span, width),
            ahead(span, width),
            ahead(span, 5 * width),
            fixed(slots, width),
            fixed(flows, width),
        ],
        scratch_shapes=[
            pltpu.VMEM((flows, width), f32),
            pltpu.VMEM((slots, width), f32),
            pltpu.VMEM((span, 3 * width), f32),
            pltpu.VMEM((span, width), bf),
        ],
    )(fetched, path_in[0], slot_col, slot_row, lens_col, gru_wx, gru_wh, gru_bias[None])
    link_out, direct, returned, grad_w, grad_b = call(
        link_kernel,
        [
            ((links, width), bf),
            ((links, width), f32),
            ((slots, width), bf),
            ((3 * width * width // LANES, LANES), bf),
            ((8, LANES), f32),
        ],
        collective_id=1,
        in_specs=[whole()] * 10,
        out_specs=[whole()] * 5,
        scratch_shapes=[
            pltpu.VMEM((slots, width), bf),
            pltpu.VMEM((slots, width), bf),
            pltpu.SemaphoreType.DMA((2, peers)),
            pltpu.SemaphoreType.DMA((2, peers)),
        ],
    )(
        partial_value,
        serve_row,
        serve_col,
        link_rows,
        link_grad[0],
        keep_col,
        mlp_w1,
        mlp_b1[None],
        mlp_w2,
        mlp_b2[None],
    )
    dpart, path_back, grad_wx, grad_wh, grad_bias = call(
        functools.partial(backward_kernel, steps),
        grad_shapes(slots, flows, width),
        grid=(blocks,),
        in_specs=[
            fixed(slots, width),
            fixed(flows, width),
            behind(span, 1),
            behind(1, 1, span),
            fixed(flows, 1),
            fixed(width, 3 * width),
            fixed(width, 3 * width),
            behind(span, width),
            behind(span, width),
            behind(span, 5 * width),
        ],
        out_specs=[fixed(*shape) for shape, _ in grad_shapes(slots, flows, width)],
        scratch_shapes=[
            pltpu.VMEM((flows, width), f32),
            pltpu.VMEM((slots, width), f32),
            pltpu.VMEM((span, width), f32),
            pltpu.VMEM((span, 3 * width), bf),
            pltpu.VMEM((span, 3 * width), bf),
            pltpu.VMEM((width, 3 * width), f32),
            pltpu.VMEM((width, 3 * width), f32),
            pltpu.VMEM((8, 3 * width), f32),
        ],
    )(
        returned,
        path_grad[0],
        slot_col,
        slot_row,
        lens_col,
        gru_wx,
        gru_wh,
        xs,
        hs,
        coef,
    )
    devices = lax.axis_size("replica") * lax.axis_size("outer") * lax.axis_size("link")
    scale = float(devices * links) ** (-0.5)
    rows = grad_w.shape[0]
    padded = -(-rows // (16 * devices)) * 16 * devices
    grads = [grad_wx, grad_wh, grad_w]
    if padded != rows:
        grads = [jnp.pad(grad, ((0, padded - rows), (0, 0))) for grad in grads]
    owned, sums, biases = call(
        tail_kernel,
        [((slots, width), bf), ((3, padded, LANES), bf), ((16, LANES), f32)],
        collective_id=2,
        in_specs=[whole()] * 6,
        out_specs=[whole()] * 3,
        scratch_shapes=tail_scratch(padded),
    )(dpart, *grads, grad_bias, grad_b)
    link_back, total_wx, total_wh, total_b, total_w1, total_b1, total_w2, total_b2 = call(
        functools.partial(collect_kernel, scale),
        [
            ((links, width), f32),
            ((width, 3 * width), f32),
            ((width, 3 * width), f32),
            ((1, 3 * width), f32),
            ((2 * width, width), f32),
            ((1, width), f32),
            ((width, width), f32),
            ((1, width), f32),
        ],
        in_specs=[whole()] * 5,
        out_specs=[whole()] * 8,
    )(owned, serve_row, direct, sums, biases)
    return (
        link_out[None],
        path_out[None],
        link_back[None],
        path_back[None],
        total_wx,
        total_wh,
        total_b[0],
        total_w1,
        total_b1[0],
        total_w2,
        total_b2[0],
    )


def solution(mesh):
    return jax.shard_map(
        body,
        mesh=mesh,
        in_specs=(
            P("replica", ("outer", "link"), None),
            P("replica", ("outer", "link"), None),
            P("replica", ("outer", "link"), None),
            P("replica", ("outer", "link")),
            P("replica", ("outer", "link")),
            P("replica", None, ("outer", "link"), None),
            P("replica", ("outer", "link"), None),
            P("replica", ("outer", "link"), None),
            P(),
            P(),
            P(),
            P(),
            P(),
            P(),
            P(),
        ),
        out_specs=(
            P("replica", ("outer", "link"), None),
            P("replica", ("outer", "link"), None),
            P("replica", ("outer", "link"), None),
            P("replica", ("outer", "link"), None),
            P(),
            P(),
            P(),
            P(),
            P(),
            P(),
            P(),
        ),
        check_vma=False,
    )
```
